128 devices in a mesh: ckpt: 4 (over z_hi, core), fsdp: 32 (over x, y, z_lo).
Axes of the slice: x: 4, y: 4, z: 4 (z_hi: 2, z_lo: 2; z = z_hi * 2 + z_lo), core: 2. Of those that a mesh axis runs over, the one named last changes fastest.
Arguments:
- train_acts: bfloat16 [4, 4096, 4096], P('ckpt', 'fsdp'), may hold values from -6 to 6
- train_len: int32 [32, 2], replicated, may hold values from 16 to 64
- query_acts: bfloat16 [4, 256, 4096], P('ckpt', 'fsdp'), may hold values from -6 to 6
- query_len: int32 [2, 2], replicated, may hold values from 16 to 64
- norm_gain: bfloat16 [4, 4096], P('ckpt'), may hold values from 0.099609375 to 1.8984375
- up_weight: bfloat16 [4, 4096, 20480], P('ckpt', None, 'fsdp'), may hold values from -0.09375 to 0.09375
- readout: bfloat16 [4, 20480], P('ckpt', 'fsdp'), may hold values from -0.4 to 0.4
- lr_weight: float32 [4], P('ckpt'), may hold values from 0.25 to 1
Outputs:
- influence: float32 [32, 2], P('fsdp')
The draws below stay inside these ranges and needn't reach their ends.
All inputs are finite; a program needn't handle non-finite values.
Results may differ from the reference program's by a relative error of at most 0.0055.
Values may be sent and summed in bfloat16 or wider, within the bound.
No kernel may reach another device: no remote copies, remote signals or barrier semaphores. Data moves between devices by JAX's collectives and lax.ppermute only.
A program may use at most 128 MiB of HBM per device.

```python
import math
import jax
import jax.numpy as jnp
from jax import lax

D = 4096
FF = 20480
LEN = 64
QPAIRS = 2
CKPTS = 4
PAIRS = 32
TTOK = 4096
QTOK = 256


def draw_readout(key, part):
    key = jax.random.fold_in(key, 7)
    position = jnp.arange(FF, dtype=jnp.float32) / float(FF)
    profile = 0.004 * jnp.exp(position * (1.5 * math.log(10.0)))
    noise = jnp.clip(jax.random.normal(key, (CKPTS, FF), jnp.float32), -3.0, 3.0)
    return (profile[None, :] * noise).astype(jnp.bfloat16)


def touch_ends(result, rng, low, high):
    longest = result.shape.index(max(result.shape))
    spots = []
    for shift in (0, 1):
        where = [jax.random.randint(jax.random.fold_in(rng, axis), (), 0, length) for axis, length in enumerate(result.shape)]
        where[longest] = (where[longest] + shift) % result.shape[longest]
        spots.append(tuple(where))
    return result.at[spots[0]].set(low).at[spots[1]].set(high)


def block_levels(rng, dims, shards, least, high):
    factor_of = 1.0
    for dim, parts in shards:
        steps = jax.random.uniform(jax.random.fold_in(jax.random.fold_in(rng, 6), dim), (parts,), jnp.float32, least / len(shards), high / len(shards))
        factor_of = factor_of * jnp.repeat(jnp.exp(steps), dims[dim] // parts).reshape((-1,) + (1,) * (len(dims) - 1 - dim))
    return factor_of


def gaussian(key, dims, spread, most, split=(), held_as=jnp.bfloat16):
    entries = spread * jax.random.normal(key, dims, jnp.float32)
    if split:
        entries = entries * block_levels(key, dims, split, -0.22, 0.18)
    return jnp.clip(entries, -most, most).astype(held_as)


def setup_inputs(seed: int = 0) -> dict:
    key_list = jax.random.split(jax.random.key(seed), 9)
    return {
        "train_acts": gaussian(key_list[0], (CKPTS, TTOK, D), 1.0, 6.0, ((0, 4), (1, 32))),
        "train_len": touch_ends(jax.random.randint(key_list[1], (PAIRS, 2), LEN // 4, LEN + 1), jax.random.fold_in(key_list[1], 1), LEN // 4, LEN).astype(jnp.int32),
        "query_acts": gaussian(key_list[2], (CKPTS, QTOK, D), 1.0, 6.0, ((0, 4), (1, 32))),
        "query_len": touch_ends(jax.random.randint(key_list[3], (QPAIRS, 2), LEN // 4, LEN + 1), jax.random.fold_in(key_list[3], 1), LEN // 4, LEN).astype(jnp.int32),
        "norm_gain": jnp.clip(1.0 + 0.18 * jax.random.normal(key_list[4], (CKPTS, D), jnp.float32), 0.099609375, 1.8984375).astype(jnp.bfloat16),
        "up_weight": gaussian(key_list[5], (CKPTS, D, FF), D ** -0.5, 0.09375, ((0, 4), (2, 32))),
        "readout": draw_readout(jax.random.fold_in(key_list[8], 71), 0),
        "lr_weight": jnp.clip(jnp.exp(math.log(1.0) - 1.3862944 * jax.random.uniform(key_list[7], (CKPTS,), jnp.float32) ** block_levels(key_list[7], (CKPTS,), ((0, 4),), -0.2, 0.2)), 0.25, 1.0),
    }


def normalize(values_in, gain_row):
    values = values_in.astype(jnp.float32)
    scale = lax.rsqrt(lax.optimization_barrier(jnp.mean(values * values, axis=-1, keepdims=True)) + 1e-05)
    return (values * scale * gain_row.astype(jnp.float32)).astype(jnp.bfloat16)

def token_weights(lengths):
    positions = jnp.arange(LEN, dtype=jnp.int32)
    live = (positions[None, None, :] < lengths[:, :, None]).astype(jnp.float32)
    return (live / lengths[:, :, None].astype(jnp.float32)).reshape(-1)

def seq_rewards(hidden, head, weights, count):
    terms = jnp.dot(jax.nn.silu(hidden), head.astype(jnp.float32), precision=lax.Precision.HIGHEST)
    return (terms * weights).reshape(count, 2, LEN).sum(axis=-1)

def token_slopes(rewards):
    slope = jax.nn.sigmoid(rewards[:, 1] - rewards[:, 0])
    signed = jnp.stack([-slope, slope], axis=1)
    return (signed[:, :, None] * jnp.ones((1, 1, LEN), jnp.float32)).reshape(-1)

def out_grads(hidden, head, factor):
    sig = jax.nn.sigmoid(hidden)
    deriv = sig * (1.0 + hidden * (1.0 - sig))
    return (factor[:, None] * head.astype(jnp.float32)[None, :] * deriv).astype(jnp.bfloat16)

def reference(train_acts, train_len, query_acts, query_len, norm_gain, up_weight, readout, lr_weight):
    pairs = train_len.shape[0]
    train_weight = token_weights(train_len)
    query_weight = token_weights(query_len)
    total = jnp.zeros((pairs, QPAIRS), jnp.float32)
    for checkpoint in range(CKPTS):
        normed = normalize(train_acts[checkpoint], norm_gain[checkpoint])
        query_normed = normalize(query_acts[checkpoint], norm_gain[checkpoint])
        weight = up_weight[checkpoint].astype(jnp.float32)
        hidden = jnp.dot(normed.astype(jnp.float32), weight, precision=lax.Precision.HIGHEST)
        query_hidden = jnp.dot(query_normed.astype(jnp.float32), weight, precision=lax.Precision.HIGHEST)
        head = readout[checkpoint]
        train_reward = seq_rewards(hidden, head, train_weight, pairs)
        query_reward = seq_rewards(query_hidden, head, query_weight, QPAIRS)
        grad_out = out_grads(hidden, head, token_slopes(train_reward) * train_weight)
        query_grad = out_grads(query_hidden, head, token_slopes(query_reward) * query_weight)
        input_gram = jnp.dot(normed.astype(jnp.float32), query_normed.astype(jnp.float32).T, precision=lax.Precision.HIGHEST)
        output_gram = jnp.dot(grad_out.astype(jnp.float32), query_grad.astype(jnp.float32).T, precision=lax.Precision.HIGHEST)
        scores = (input_gram * output_gram).reshape(pairs, 2 * LEN, QPAIRS, 2 * LEN).sum(axis=(1, 3))
        total = total + lr_weight[checkpoint] * scores
    return total
```

```python
import functools

import jax
import jax.numpy as jnp
from jax import lax
from jax.experimental import pallas as pl
from jax.experimental.pallas import tpu as pltpu
from jax.sharding import Mesh
from jax.sharding import PartitionSpec as P

LEN = 64
D = 4096
FD = 640
TILES = 5
NQ = 256
OFFS = (0, -1, 1, 2)
F32 = jnp.float32
BF16 = jnp.bfloat16


def ring(step):
    return [(i, (i + step) % 4) for i in range(4)]


def normalize(values_in, gain_row):
    values = values_in.astype(F32)
    scale = lax.rsqrt(jnp.mean(values * values, axis=-1, keepdims=True) + 1e-05)
    return (values * scale * gain_row.astype(F32)).astype(BF16)


def start_weights(wt, we, ws, sems):
    copies = []
    for j in range(TILES):
        cols = pl.ds(128 * j, 128)
        a = pltpu.make_async_copy(wt.at[:, cols], ws.at[j, :, pl.ds(0, 128)], sems.at[j, 0])
        b = pltpu.make_async_copy(we.at[:, cols], ws.at[j, :, pl.ds(128, 128)], sems.at[j, 1])
        a.start()
        b.start()
        copies.append((a, b))
    return copies


def activations(h):
    sig = 0.5 * jnp.tanh(0.5 * h) + 0.5
    act = h * sig
    return act, sig + act * (1.0 - sig)


def query_kernel(qa, qb, wt, we, head, qg_out, terms_out, xs, ws, acc, xsem, wsem):
    ca = pltpu.make_async_copy(qa, xs.at[pl.ds(0, 128)], xsem.at[0])
    cb = pltpu.make_async_copy(qb, xs.at[pl.ds(128, 128)], xsem.at[1])
    ca.start()
    cb.start()
    copies = start_weights(wt, we, ws, wsem)
    ca.wait()
    cb.wait()
    acc[...] = jnp.zeros_like(acc)
    for j in range(TILES):
        copies[j][0].wait()
        copies[j][1].wait()
        h = jnp.dot(xs[...], ws[j], preferred_element_type=F32)
        act, deriv = activations(h)
        row = head[:, 256 * j:256 * (j + 1)]
        acc[...] += act * row
        qg_out[:, 256 * j:256 * (j + 1)] = (row * row * deriv).astype(BF16)
    terms_out[...] = jnp.sum(acc[...], axis=1, keepdims=True)


def train_kernel(rows, *refs):
    n = len(rows)
    total = sum(rows)
    xin = refs[:n]
    lens, wt, we, qa, qb, qg, head, r_out, z_out, xs, qs, ws, acc, gram, xsem, qsem, wsem = refs[n:]
    xcopies = []
    at = 0
    for i in range(n):
        c = pltpu.make_async_copy(xin[i], xs.at[pl.ds(at, rows[i])], xsem.at[i])
        c.start()
        xcopies.append(c)
        at += rows[i]
    copies = start_weights(wt, we, ws, wsem)
    ca = pltpu.make_async_copy(qa, qs.at[pl.ds(0, 128)], qsem.at[0])
    cb = pltpu.make_async_copy(qb, qs.at[pl.ds(128, 128)], qsem.at[1])
    ca.start()
    cb.start()
    for c in xcopies:
        c.wait()
    acc[...] = jnp.zeros_like(acc)
    gram[...] = jnp.zeros_like(gram)
    for j in range(TILES):
        copies[j][0].wait()
        copies[j][1].wait()
        row = head[:, 256 * j:256 * (j + 1)]

        @pl.loop(0, total // 256)
        def _(k, j=j, row=row):
            part = pl.ds(pl.multiple_of(k * 256, 256), 256)
            h = jnp.dot(xs[part, :], ws[j], preferred_element_type=F32)
            act, deriv = activations(h)
            acc[part, :] += act * row
            gram[part, :] += lax.dot_general(
                deriv.astype(BF16), qg[:, 256 * j:256 * (j + 1)], (((1,), (1,)), ((), ())), preferred_element_type=F32
            )
    ca.wait()
    cb.wait()

    @pl.loop(0, total // 256)
    def _(k):
        part = pl.ds(pl.multiple_of(k * 256, 256), 256)
        gram[part, :] = gram[part, :] * lax.dot_general(
            xs[part, :], qs[...], (((1,), (1,)), ((), ())), preferred_element_type=F32
        )

    position = lax.broadcasted_iota(jnp.int32, (LEN, 1), 0)
    for s in range(total // LEN):
        length = lens[s]
        weight = jnp.where(position < length, 1.0 / length.astype(F32), 0.0)
        r_out[s:s + 1, :] = jnp.sum(acc[LEN * s:LEN * (s + 1), :] * weight, axis=0, keepdims=True)
        z_out[s:s + 1, :] = jnp.sum(gram[LEN * s:LEN * (s + 1), :] * weight, axis=0, keepdims=True)


ANY = pl.BlockSpec(memory_space=pl.ANY)
VM = pl.BlockSpec(memory_space=pltpu.VMEM)
SM = pl.BlockSpec(memory_space=pltpu.SMEM)


def query_call(qa, qb, wt, we, head):
    return pl.pallas_call(
        query_kernel,
        out_shape=(jax.ShapeDtypeStruct((NQ, 2 * FD), BF16), jax.ShapeDtypeStruct((NQ, 1), F32)),
        in_specs=[ANY, ANY, ANY, ANY, VM],
        out_specs=(VM, VM),
        scratch_shapes=[
            pltpu.VMEM((NQ, D), BF16),
            pltpu.VMEM((TILES, D, 256), BF16),
            pltpu.VMEM((NQ, 256), F32),
            pltpu.SemaphoreType.DMA((2,)),
            pltpu.SemaphoreType.DMA((TILES, 2)),
        ],
        compiler_params=pltpu.CompilerParams(vmem_limit_bytes=40 * 2**20),
        cost_estimate=pl.CostEstimate(flops=2 * NQ * D * 2 * FD, bytes_accessed=13 * 2**20, transcendentals=NQ * 2 * FD),
        name="query_side",
    )(qa, qb, wt, we, head)


def train_call(xin, lens, wt, we, qa, qb, qg, head):
    rows = tuple(x.shape[0] for x in xin)
    total = sum(rows)
    return pl.pallas_call(
        functools.partial(train_kernel, rows),
        out_shape=(jax.ShapeDtypeStruct((total // LEN, 256), F32),) * 2,
        in_specs=[ANY] * len(rows) + [SM, ANY, ANY, ANY, ANY, VM, VM],
        out_specs=(VM, VM),
        scratch_shapes=[
            pltpu.VMEM((total, D), BF16),
            pltpu.VMEM((NQ, D), BF16),
            pltpu.VMEM((TILES, D, 256), BF16),
            pltpu.VMEM((total, 256), F32),
            pltpu.VMEM((total, 256), F32),
            pltpu.SemaphoreType.DMA((len(rows),)),
            pltpu.SemaphoreType.DMA((2,)),
            pltpu.SemaphoreType.DMA((TILES, 2)),
        ],
        compiler_params=pltpu.CompilerParams(vmem_limit_bytes=40 * 2**20),
        cost_estimate=pl.CostEstimate(
            flops=2 * total * D * (2 * FD + NQ), bytes_accessed=13 * 2**20 + total * D * 2, transcendentals=total * 2 * FD
        ),
        name="train_side",
    )(*xin, lens, wt, we, qa, qb, qg, head)


def ring_gather_start(block, axis):
    low = lax.ppermute(block, axis, ring(1))
    high = lax.ppermute(block, axis, ring(-1))
    return low, high


def ring_gather_finish(low, high, axis):
    half = low.shape[0] // 2
    far_a = lax.ppermute(low[:half], axis, ring(1))
    far_b = lax.ppermute(high[half:], axis, ring(-1))
    return far_a, far_b


def local(train_acts, train_len, query_acts, query_len, norm_gain, up_weight, readout, lr_weight):
    core = lax.axis_index("c")
    turn = functools.partial(lax.ppermute, axis_name=("c", "zl"), perm=[(0, 0), (1, 2), (2, 1), (3, 3)])
    swap = functools.partial(lax.ppermute, axis_name="c", perm=[(0, 1), (1, 0)])

    normed = normalize(train_acts[0], norm_gain[0])
    query_own = normalize(query_acts[0], norm_gain[0])
    own = turn(normed)
    query_turned = turn(query_own)
    small = jnp.concatenate([readout[0].astype(F32), lr_weight, jnp.zeros((127,), F32)]).reshape(1, FD + 128)
    small = turn(small)
    small_other = swap(small)
    lr = small[0, FD]
    head = jnp.stack(
        [small[0, :FD].reshape(TILES, 128), small_other[0, :FD].reshape(TILES, 128)], axis=1
    ).reshape(1, 2 * FD)

    weight_in, own = lax.optimization_barrier((up_weight[0], own))
    wt = turn(weight_in)
    we = swap(wt)
    qa = lax.all_gather(query_turned, ("x", "y"), axis=0, tiled=True)
    qb = swap(qa)

    one, two = own[:LEN], own[LEN:]
    one_low, one_high = ring_gather_start(one, "x")
    two_low, two_high = ring_gather_start(two, "y")
    one_a, one_b = ring_gather_finish(one_low, one_high, "x")
    two_a, two_b = ring_gather_finish(two_low, two_high, "y")
    g1 = jnp.concatenate([one, one_low, one_high, one_a, one_b], axis=0)
    g2 = jnp.concatenate([two, two_low, two_high, two_a, two_b], axis=0)
    g1_low, g1_high = ring_gather_start(g1, "y")
    g2_low, g2_high = ring_gather_start(g2, "x")
    g1_a, g1_b = ring_gather_finish(g1_low, g1_high, "y")
    g2_a, g2_b = ring_gather_finish(g2_low, g2_high, "x")

    lens = lax.dynamic_index_in_dim(train_len.reshape(4, 4, 2, 2), core, 2, keepdims=False)
    places = jnp.array(OFFS, jnp.int32)
    lens = jnp.take(lens, (places + lax.axis_index("x")) % 4, axis=0)
    lens = jnp.take(lens, (places + lax.axis_index("y")) % 4, axis=1)

    i = jnp.arange(NQ, dtype=jnp.int32)
    side = jnp.where(i < 128, core, 1 - core)
    inner = i % 128
    qseq = inner // 32
    qpos = 16 * ((inner // 8) % 4) + 8 * side + inner % 8
    qlen = jnp.take(query_len.reshape(-1), qseq)
    qw = jnp.where(qpos < qlen, 1.0 / qlen.astype(F32), 0.0)
    pick = (qseq[:, None] == jnp.arange(4)[None, :]).astype(F32) * qw[:, None]

    qg, qterms = query_call(qa, qb, wt, we, head)
    qreward = jnp.sum(qterms * pick, axis=0)

    run = lambda xin, ls: train_call(xin, ls, wt, we, qa, qb, qg, head)
    r_c, z_c = run((g1, g2), jnp.concatenate([lens[:, 0, 0], lens[0, :, 1]]))
    r_1, z_1 = run((g1_low, g1_high), jnp.concatenate([lens[:, 1, 0], lens[:, 2, 0]]))
    r_2, z_2 = run((g2_low, g2_high), jnp.concatenate([lens[1, :, 1], lens[2, :, 1]]))
    r_f, z_f = run((g1_a, g1_b, g2_a, g2_b), jnp.concatenate([lens[:, 3, 0], lens[3, :, 1]]))
    order = lambda c, a, b, f: jnp.stack(
        [
            jnp.stack([c[:4], a[:4], a[4:], f[:4]], axis=1),
            jnp.stack([c[4:], b[:4], b[4:], f[4:]], axis=0),
        ]
    )
    rewards = jnp.sum(order(r_c, r_1, r_2, r_f), axis=-1, keepdims=True)
    scores = jnp.sum(order(z_c, z_1, z_2, z_f)[..., None] * pick, axis=-2)
    values = jnp.concatenate([rewards, scores], axis=-1)

    def spread(parts, query, axis):
        sent = [jnp.concatenate([p.reshape(1, -1), query.reshape(1, -1)], axis=1) for p in parts]
        total = sent[0]
        for k in (1, 2, 3):
            total = total + lax.ppermute(sent[k], axis, ring(OFFS[k]))
        return total[0, :-4].reshape(parts[0].shape), total[0, -4:]

    values, qreward = spread([values[:, k] for k in range(4)], qreward, "x")
    values, qreward = spread([values[:, k] for k in range(4)], qreward, "y")

    slope = jax.nn.sigmoid(values[1, 0] - values[0, 0])
    qr = qreward.reshape(2, 2)
    qslope = jax.nn.sigmoid(qr[:, 1] - qr[:, 0])
    by_query = (slope * (values[1, 1:] - values[0, 1:])).reshape(2, 2)
    mine = lr * qslope * (by_query[:, 1] - by_query[:, 0])
    mine = jnp.concatenate([mine, jnp.zeros((126,), F32)]).reshape(1, 128)
    total = jnp.zeros((1, 128), F32)
    for a in (0, 1):
        for b in (0, 1):
            perm = []
            for zh in (0, 1):
                for q in (0, 1):
                    for c in (0, 1):
                        perm.append((4 * (zh ^ a) + 2 * q + (c ^ b), 4 * zh + 2 * c + q))
            total = total + lax.ppermute(mine, ("zh", "c", "zl"), perm)
    return total[:, :2]


def solution(mesh):
    full = Mesh(mesh.devices.reshape(2, 2, 4, 4, 2), ("zh", "c", "x", "y", "zl"))
    ckpt, fsdp = ("zh", "c"), ("x", "y", "zl")
    return jax.shard_map(
        local,
        mesh=full,
        in_specs=(
            P(ckpt, fsdp, None),
            P(),
            P(ckpt, fsdp, None),
            P(),
            P(ckpt, None),
            P(ckpt, None, fsdp),
            P(ckpt, fsdp),
            P(ckpt),
        ),
        out_specs=P(fsdp, None),
        check_vma=False,
    )
```

```python
import functools

import jax
import jax.numpy as jnp
from jax import lax
from jax.experimental import pallas as pl
from jax.experimental.pallas import tpu as pltpu
from jax.sharding import Mesh
from jax.sharding import PartitionSpec as P

LEN = 64
D = 4096
FD = 640
TILES = 5
NQ = 256
OFFS = (0, -1, 1, 2)
F32 = jnp.float32
BF16 = jnp.bfloat16
NT = (((1,), (1,)), ((), ()))
HIGHEST = lax.Precision.HIGHEST
CP = 48
HEAD = LEN - CP
REWARD, SECOND, QUERY, RATE = 4, 8, 16, 20


def ring(step):
    return [(i, (i + step) % 4) for i in range(4)]


def activations(h):
    sig = 0.5 * jnp.tanh(0.5 * h) + 0.5
    act = h * sig
    return act, sig + act * (1.0 - sig)


def fold(v):
    return v[:, :128] + v[:, 128:]


def norm_kernel(acts, query, gain, one, two, rest, qown):
    def norm(v):
        v = v.astype(F32)
        scale = lax.rsqrt(jnp.mean(v * v, axis=-1, keepdims=True) + 1e-05)
        return (v * scale * gain[...].astype(F32)).astype(BF16)

    one[...] = norm(acts[HEAD:LEN, :])
    two[...] = norm(acts[LEN + HEAD:, :])
    rest[0:HEAD, :] = norm(acts[:HEAD, :])
    rest[HEAD:2 * HEAD, :] = norm(acts[LEN:LEN + HEAD, :])
    qown[...] = norm(query[...])


def norm_call(acts, query, gain):
    return pl.pallas_call(
        norm_kernel,
        out_shape=tuple(jax.ShapeDtypeStruct((n, D), BF16) for n in (CP, CP, 2 * HEAD, 8)),
        in_specs=[VM] * 3,
        out_specs=(VM,) * 4,
        cost_estimate=pl.CostEstimate(flops=4 * 136 * D, bytes_accessed=4 * 2**20, transcendentals=136),
        name="norm_rows",
    )(acts, query, gain)


def copy_kernel(moves, n, m, *refs):
    src, dst, sem = refs[:n], refs[n:n + m], refs[n + m]
    copies = [
        pltpu.make_async_copy(src[i].at[pl.ds(s, k)], dst[o].at[pl.ds(d, k)], sem.at[c])
        for c, (i, s, o, d, k) in enumerate(moves)
    ]
    for c in copies:
        c.start()
    for c in copies:
        c.wait()


def copy_call(parts, rows, moves, name):
    return pl.pallas_call(
        functools.partial(copy_kernel, moves, len(parts), len(rows)),
        out_shape=tuple(jax.ShapeDtypeStruct((n, D), BF16) for n in rows),
        in_specs=[ANY] * len(parts),
        out_specs=(VM,) * len(rows),
        scratch_shapes=[pltpu.SemaphoreType.DMA((len(moves),))],
        cost_estimate=pl.CostEstimate(flops=0, bytes_accessed=sum(rows) * D * 4, transcendentals=0),
        name=name,
    )(*parts)


def rows_kernel(shapes, block, with_queries, *refs):
    n = len(shapes)
    xin = refs[:n]
    info, train_len, query_len, queries, own, first, second = refs[n:n + 7]
    if with_queries:
        small, small_first, small_second, out, qg, heads = refs[n + 7:n + 13]
    else:
        before, qg, heads, out = refs[n + 7:n + 11]
    xs, qs, ws, dv, acc, gram, sums_r, sums_z, xsem, qsem, wsem = refs[-11:]
    straight = info[0] == 1
    x, y, core = info[1], info[2], info[3]

    starts, at = [], 0
    for rows, _ in shapes:
        starts.append(at)
        at += rows
    total = at
    xloads = [
        pltpu.make_async_copy(xin[i], xs.at[pl.ds(starts[i], shapes[i][0])], xsem.at[i]) for i in range(n)
    ]

    u = lax.broadcasted_iota(jnp.int32, (NQ, 128), 0)
    lane = lax.broadcasted_iota(jnp.int32, (NQ, 128), 1)
    qx, qy = (u >> 5) & 3, (u >> 3) & 3
    position = 8 * (2 * qy + jnp.where(u < 128, 1, 0)) + (u & 7)
    length = jnp.zeros((NQ, 128), jnp.int32)
    for k in range(4):
        length = jnp.where(qx == k, query_len[k // 2, k % 2], length)
    weight = jnp.where(position < length, 1.0 / jnp.maximum(length, 1).astype(F32), 0.0)

    def pick(at):
        return jnp.where(qx == lane - at, weight, 0.0)

    qload = pltpu.make_async_copy(queries, qs, qsem)

    def tiles(a, b):
        moves = []
        for j in range(TILES):
            cols = pl.ds(128 * j, 128)
            for h, side in enumerate((a, b)):
                dst = ws.at[j, :, pl.ds(128 * h, 128)]
                moves.append(pltpu.make_async_copy(side.at[:, cols], dst, wsem.at[j, h]))
        return moves

    def start_tiles():
        @pl.when(straight)
        def _():
            for c in tiles(own, first):
                c.start()

        @pl.when(jnp.logical_not(straight))
        def _():
            for c in tiles(first, second):
                c.start()

    def wait_tiles():
        for c in tiles(first, second):
            c.wait()

    qload.start()
    if with_queries:
        start_tiles()
        for j in range(TILES):
            cols = slice(128 * j, 128 * (j + 1))
            heads[:, 256 * j:256 * j + 128] = jnp.where(straight, small[:, cols], small_first[:, cols])
            heads[:, 256 * j + 128:256 * j + 256] = jnp.where(straight, small_first[:, cols], small_second[:, cols])
        qload.wait()
        wait_tiles()
        for c in xloads:
            c.start()
        query_total = None
        for j in range(TILES):
            row = heads[:, 256 * j:256 * (j + 1)]
            act, deriv = activations(jnp.dot(qs[...], ws[j], preferred_element_type=F32))
            part = fold(act * row)
            query_total = part if j == 0 else query_total + part
            qg[:, 256 * j:256 * (j + 1)] = (row * row * deriv).astype(BF16)
        common = jnp.sum(jnp.sum(query_total, axis=1, keepdims=True) * pick(QUERY), axis=0, keepdims=True)
        common += jnp.where(straight, small[:, FD:], small_first[:, FD:])
        out[...] = jnp.broadcast_to(common, (16, 128))
        for c in xloads:
            c.wait()
    else:
        for c in xloads:
            c.start()
        out[...] = before[...]
        qload.wait()
        for c in xloads:
            c.wait()
        start_tiles()

    @pl.loop(0, total // block)
    def _(b):
        at = pl.ds(pl.multiple_of(b * block, block), block)
        gram[at, :] = lax.dot_general(xs[at, :], qs[...], NT, preferred_element_type=F32)

    if not with_queries:
        wait_tiles()

    @pl.loop(0, total // block)
    def _(b):
        at = pl.ds(pl.multiple_of(b * block, block), block)
        for j in range(TILES):
            cols = slice(256 * j, 256 * (j + 1))
            act, deriv = activations(jnp.dot(xs[at, :], ws[j], preferred_element_type=F32))
            part = fold(act * heads[:, cols])
            if j == 0:
                acc[at, :] = part
            else:
                acc[at, :] += part
            dv[:, cols] = deriv.astype(BF16)
        gram[at, :] = gram[at, :] * lax.dot_general(dv[...], qg[...], NT, preferred_element_type=F32)

    runs = []
    for i, (_, found) in enumerate(shapes):
        for row, count, side, relative, gx, gy, slot in found:
            place = lax.rem(x + gx + 4, 4) * 4 + lax.rem(y + gy + 4, 4) if relative else 4 * gx + gy
            runs.append((starts[i] + row, count, side, place, slot))
    for k, (row, count, side, place, slot) in enumerate(runs):
        length = train_len[place * 2 + 1 - core, side]
        live = lax.broadcasted_iota(jnp.int32, (count, 1), 0) + slot < length
        live = jnp.where(live, 1.0 / jnp.maximum(length, 1).astype(F32), 0.0)
        sums_r[k:k + 1, :] = jnp.sum(acc[row:row + count, :] * live, axis=0, keepdims=True)
        sums_z[k:k + 1, :] = jnp.sum(gram[row:row + count, :] * live, axis=0, keepdims=True)
    reward = jnp.sum(sums_r[...], axis=1, keepdims=True)
    lanes = lax.broadcasted_iota(jnp.int32, (len(runs), 128), 1)
    tables = []
    for at in (0, SECOND):
        scores = jnp.dot(sums_z[...], pick(at), precision=HIGHEST, preferred_element_type=F32)
        tables.append(scores + jnp.where(lanes == at + REWARD, reward, 0.0))
    for k, (_, _, side, place, _) in enumerate(runs):
        at = pl.ds(place, 1)
        out[at, :] = out[at, :] + tables[side][k:k + 1, :]


ANY = pl.BlockSpec(memory_space=pl.ANY)
HBM = pl.BlockSpec(memory_space=pltpu.HBM)
VM = pl.BlockSpec(memory_space=pltpu.VMEM)
SM = pl.BlockSpec(memory_space=pltpu.SMEM)


def rows_call(rows, block, name, given, with_queries):
    xin = [r[0] for r in rows]
    shapes = tuple((v.shape[0], found) for v, found in rows)
    n, total = len(rows), sum(v.shape[0] for v in xin)
    runs = sum(len(found) for _, found in rows)
    out_shape = [jax.ShapeDtypeStruct((16, 128), F32)]
    if with_queries:
        out_shape += [jax.ShapeDtypeStruct((NQ, 2 * FD), BF16), jax.ShapeDtypeStruct((1, 2 * FD), F32)]
    return pl.pallas_call(
        functools.partial(rows_kernel, shapes, block, with_queries),
        out_shape=tuple(out_shape),
        in_specs=[HBM] * n + [SM] * 3 + [HBM] * 4 + [VM] * 3,
        out_specs=(VM,) * len(out_shape),
        scratch_shapes=[
            pltpu.VMEM((total, D), BF16),
            pltpu.VMEM((NQ, D), BF16),
            pltpu.VMEM((TILES, D, 256), BF16),
            pltpu.VMEM((block, 2 * FD), BF16),
            pltpu.VMEM((total, 128), F32),
            pltpu.VMEM((total, 256), F32),
            pltpu.VMEM((runs, 128), F32),
            pltpu.VMEM((runs, 256), F32),
            pltpu.SemaphoreType.DMA((n,)),
            pltpu.SemaphoreType.DMA,
            pltpu.SemaphoreType.DMA((TILES, 2)),
        ],
        compiler_params=pltpu.CompilerParams(vmem_limit_bytes=56 * 2**20),
        cost_estimate=pl.CostEstimate(flops=1, bytes_accessed=1, transcendentals=0),
        name=name,
    )(*xin, *given)


def final_kernel(plane, got, out):
    rows = lax.broadcasted_iota(jnp.int32, (32, 128), 0)
    parts = []
    for zh in (0, 1):
        at = pl.ds(pl.multiple_of(64 * zh + 32 * (1 - plane[0]), 32), 32)
        v = got[at, :]
        for p in (0, 1):
            parts.append(jnp.sum(jnp.where((rows & 1) == p, v, 0.0), axis=0, keepdims=True))
    total = jnp.concatenate(parts, axis=0)
    lanes = lax.broadcasted_iota(jnp.int32, (4, 128), 1)
    at = lambda k: jnp.sum(jnp.where(lanes == k, total, 0.0), axis=1, keepdims=True)
    sigmoid = lambda v: 0.5 * jnp.tanh(0.5 * v) + 0.5
    factor = at(RATE) * (1.0 / 16.0) * sigmoid(at(SECOND + REWARD) - at(REWARD))
    for i in (0, 1):
        scores = [at(SECOND + 2 * i + k) - at(2 * i + k) for k in (0, 1)]
        value = factor * sigmoid(at(QUERY + 2 * i + 1) - at(QUERY + 2 * i)) * (scores[1] - scores[0])
        out[:, i:i + 1] = jnp.sum(value, axis=0, keepdims=True)


def final_call(plane, got):
    return pl.pallas_call(
        final_kernel,
        out_shape=jax.ShapeDtypeStruct((1, 2), F32),
        in_specs=[SM, VM],
        out_specs=VM,
        name="influence",
    )(plane, got)


def local(train_acts, train_len, query_acts, query_len, norm_gain, up_weight, readout, lr_weight):
    core, plane = lax.axis_index("c"), lax.axis_index("zl")
    x, y = lax.axis_index("x"), lax.axis_index("y")
    straight = core == plane
    turn = functools.partial(lax.ppermute, axis_name=("c", "zl"), perm=[(0, 2), (2, 3), (3, 1), (1, 0)])
    swap = functools.partial(lax.ppermute, axis_name="c", perm=[(0, 1), (1, 0)])
    low = lambda v, axis: lax.ppermute(v, axis, ring(1))
    high = lambda v, axis: lax.ppermute(v, axis, ring(-1))

    one, two, rest, qown = norm_call(train_acts[0], query_acts[0], norm_gain)
    small = jnp.concatenate(
        [readout[0].astype(F32), jnp.zeros((RATE,), F32), lr_weight, jnp.zeros((127 - RATE,), F32)]
    ).reshape(1, FD + 128)
    qown, small_first, one, two, rest = turn(qown), turn(small), turn(one), turn(two), turn(rest)
    weight_own, qown, small_first, one, two, rest = lax.optimization_barrier(
        (up_weight[0], qown, small_first, one, two, rest)
    )
    weight_first = turn(weight_own)
    small_second = swap(small_first)
    queries = lax.all_gather(qown, ("c", "x", "y"), axis=0, tiled=True)
    some = lax.all_gather(rest, ("x", "y"), axis=0, tiled=True)

    one_low, one_high = low(one, "x"), high(one, "x")
    two_low, two_high = low(two, "y"), high(two, "y")
    one_a, one_b = low(one_low[:32], "x"), high(one_high[32:], "x")
    two_a, two_b = low(two_low[:32], "y"), high(two_high[32:], "y")
    moves = []
    for g in (0, 1):
        moves += [(5 * g, 0, 2 * g, 0, CP), (5 * g + 1, 0, 2 * g, CP, CP), (5 * g + 2, 0, 2 * g + 1, 0, CP),
                  (5 * g + 3, 0, 2 * g + 1, CP, 32), (5 * g + 4, 0, 2 * g + 1, CP + 32, 16)]
    a1, b1, a2, b2 = copy_call(
        (one, one_low, one_high, one_a, one_b, two, two_low, two_high, two_a, two_b), (2 * CP,) * 4, moves, "join_rows"
    )
    a1_low, b1_high = low(a1, "y"), high(b1, "y")
    a2_low, b2_high = low(a2, "x"), high(b2, "x")
    weight_first, a1_low, b1_high, a2_low, b2_high = lax.optimization_barrier(
        (weight_first, a1_low, b1_high, a2_low, b2_high)
    )
    weight_second = swap(weight_first)
    b1_low, a1_high = low(b1, "y"), high(a1, "y")
    b2_low, a2_high = low(b2, "x"), high(a2, "x")
    a1_far, b1_far = low(a1_low, "y"), high(b1_high, "y")
    a2_far, b2_far = low(a2_low, "x"), high(b2_high, "x")

    def group(side, g, ks):
        found = []
        for i, k in enumerate(ks):
            gx, gy = (OFFS[k], OFFS[g]) if side == 0 else (OFFS[g], OFFS[k])
            found.append((CP * i, CP, side, True, gx, gy, HEAD))
        return tuple(found)

    gathered_runs = tuple(
        (HEAD * (2 * p + side), HEAD, side, False, p // 4, p % 4, 0) for p in range(16) for side in (0, 1)
    )
    near, rest = (0, 1), (2, 3)
    info = jnp.stack([straight.astype(jnp.int32), x, y, core])
    given = (info, train_len, query_len, queries, weight_own, weight_first, weight_second)
    sums, *kept = rows_call(
        [(a1, group(0, 0, near)), (b1, group(0, 0, rest)), (a2, group(1, 0, near)), (b2, group(1, 0, rest))],
        192, "first_rows", (*given, small, small_first, small_second), True,
    )
    (sums,) = rows_call(
        [(a1_low, group(0, 1, near)), (b1_high, group(0, 2, rest)), (a2_low, group(1, 1, near)), (b2_high, group(1, 2, rest)),
         (b1_low, group(0, 1, rest)), (a1_high, group(0, 2, near)), (b2_low, group(1, 1, rest)), (a2_high, group(1, 2, near)),
         (some, gathered_runs)],
        256, "next_rows", (*given, sums, *kept), False,
    )
    (sums,) = rows_call(
        [(a1_far, group(0, 3, near)), (b1_far, group(0, 3, rest)), (a2_far, group(1, 3, near)), (b2_far, group(1, 3, rest))],
        192, "last_rows", (*given, sums, *kept), False,
    )
    message = jnp.broadcast_to(sums.reshape(1, 16, 1, 128), (4, 16, 2, 128)).reshape(128, 128)
    got = lax.all_to_all(message, ("zh", "c", "x", "y", "zl"), split_axis=0, concat_axis=0, tiled=True)
    return final_call(plane.reshape(1), got)


def solution(mesh):
    full = Mesh(mesh.devices.reshape(2, 2, 4, 4, 2), ("zh", "c", "x", "y", "zl"))
    ckpt, fsdp = ("zh", "c"), ("x", "y", "zl")
    return jax.shard_map(
        local,
        mesh=full,
        in_specs=(
            P(ckpt, fsdp, None),
            P(),
            P(ckpt, fsdp, None),
            P(),
            P(ckpt, None),
            P(ckpt, None, fsdp),
            P(ckpt, fsdp),
            P(ckpt),
        ),
        out_specs=P(fsdp, None),
        check_vma=False,
    )
```

```python
import functools

import jax
import jax.numpy as jnp
from jax import lax
from jax.experimental import pallas as pl
from jax.experimental.pallas import tpu as pltpu
from jax.sharding import Mesh
from jax.sharding import PartitionSpec as P

LEN = 64
D = 4096
FD = 640
TILES = 5
NQ = 256
OFFS = (0, -1, 1, 2)
F32 = jnp.float32
BF16 = jnp.bfloat16
NT = (((1,), (1,)), ((), ()))
HIGHEST = lax.Precision.HIGHEST
CP = 48
HEAD = LEN - CP
REWARD, SECOND, QUERY, RATE = 4, 8, 16, 20


def ring(step):
    return [(i, (i + step) % 4) for i in range(4)]


def activations(h):
    sig = 0.5 * jnp.tanh(0.5 * h) + 0.5
    act = h * sig
    return act, sig + act * (1.0 - sig)


def fold(v):
    return v[:, :128] + v[:, 128:]


def norm(v, gain):
    v = v.astype(F32)
    scale = lax.rsqrt(jnp.mean(v * v, axis=-1, keepdims=True) + 1e-05)
    return (v * scale * gain[...].astype(F32)).astype(BF16)


def query_norm_kernel(query, gain, out):
    out[...] = norm(query[...], gain)


def norm_kernel(acts, gain, one, two, rest):
    one[...] = norm(acts[HEAD:LEN, :], gain)
    two[...] = norm(acts[LEN + HEAD:, :], gain)
    rest[0:HEAD, :] = norm(acts[:HEAD, :], gain)
    rest[HEAD:, :] = norm(acts[LEN:LEN + HEAD, :], gain)


def norm_call(body, rows, acts, gain):
    return pl.pallas_call(
        body,
        out_shape=tuple(jax.ShapeDtypeStruct((n, D), BF16) for n in rows),
        in_specs=[VM] * 2,
        out_specs=(VM,) * len(rows),
        cost_estimate=pl.CostEstimate(flops=4 * sum(rows) * D, bytes_accessed=4 * sum(rows) * D, transcendentals=sum(rows)),
        name="norm_rows",
    )(acts, gain)


def copy_kernel(moves, n, m, *refs):
    src, dst, sem = refs[:n], refs[n:n + m], refs[n + m]
    copies = [
        pltpu.make_async_copy(src[i].at[pl.ds(s, k)], dst[o].at[pl.ds(d, k)], sem.at[c])
        for c, (i, s, o, d, k) in enumerate(moves)
    ]
    for c in copies:
        c.start()
    for c in copies:
        c.wait()


def copy_call(parts, rows, moves, name):
    return pl.pallas_call(
        functools.partial(copy_kernel, moves, len(parts), len(rows)),
        out_shape=tuple(jax.ShapeDtypeStruct((n, D), BF16) for n in rows),
        in_specs=[ANY] * len(parts),
        out_specs=(VM,) * len(rows),
        scratch_shapes=[pltpu.SemaphoreType.DMA((len(moves),))],
        cost_estimate=pl.CostEstimate(flops=0, bytes_accessed=sum(rows) * D * 4, transcendentals=0),
        name=name,
    )(*parts)


def rows_kernel(shapes, block, with_queries, *refs):
    n = len(shapes)
    xin = refs[:n]
    info, queries, own, first, second = refs[n:n + 5]
    if with_queries:
        small, small_first, small_second, out, qg, heads = refs[n + 5:n + 11]
    else:
        qg, heads, out = refs[n + 5:n + 8]
    xs, qs, ws, dv, acc, gram, sums_r, sums_z, xsem, qsem, wsem = refs[-11:]
    straight = info[0] == 1
    x, y, core = info[1], info[2], info[3]

    starts, xloads, at = [], [], 0
    for i, (shape, _) in enumerate(shapes):
        starts.append(at)
        xloads.append(pltpu.make_async_copy(xin[i], xs.at[pl.ds(at, shape[0])], xsem.at[i]))
        at += shape[0]
    total = at

    u = lax.broadcasted_iota(jnp.int32, (NQ, 128), 0)
    lane = lax.broadcasted_iota(jnp.int32, (NQ, 128), 1)
    qx, qy = (u >> 5) & 3, (u >> 3) & 3
    position = 8 * (2 * qy + jnp.where(u < 128, 1, 0)) + (u & 7)
    length = jnp.zeros((NQ, 128), jnp.int32)
    for k in range(4):
        length = jnp.where(qx == k, info[4 + k], length)
    weight = jnp.where(position < length, 1.0 / jnp.maximum(length, 1).astype(F32), 0.0)

    def pick(at):
        return jnp.where(qx == lane - at, weight, 0.0)

    qload = pltpu.make_async_copy(queries, qs, qsem)

    def tiles(a, b):
        moves = []
        for j in range(TILES):
            cols = pl.ds(128 * j, 128)
            for h, side in enumerate((a, b)):
                dst = ws.at[j, :, pl.ds(128 * h, 128)]
                moves.append(pltpu.make_async_copy(side.at[:, cols], dst, wsem.at[j, h]))
        return moves

    def start_tiles():
        @pl.when(straight)
        def _():
            for c in tiles(own, first):
                c.start()

        @pl.when(jnp.logical_not(straight))
        def _():
            for c in tiles(first, second):
                c.start()

    def wait_tiles():
        for c in tiles(first, second):
            c.wait()

    qload.start()
    if with_queries:
        start_tiles()
        for j in range(TILES):
            cols = slice(128 * j, 128 * (j + 1))
            heads[:, 256 * j:256 * j + 128] = jnp.where(straight, small[:, cols], small_first[:, cols])
            heads[:, 256 * j + 128:256 * j + 256] = jnp.where(straight, small_first[:, cols], small_second[:, cols])
        qload.wait()
        wait_tiles()
        for c in xloads:
            c.start()
        query_total = None
        for j in range(TILES):
            row = heads[:, 256 * j:256 * (j + 1)]
            act, deriv = activations(jnp.dot(qs[...], ws[j], preferred_element_type=F32))
            part = fold(act * row)
            query_total = part if j == 0 else query_total + part
            qg[:, 256 * j:256 * (j + 1)] = (row * row * deriv).astype(BF16)
        common = jnp.sum(jnp.sum(query_total, axis=1, keepdims=True) * pick(QUERY), axis=0, keepdims=True)
        common += jnp.where(straight, small[:, FD:], small_first[:, FD:])
        out[...] = jnp.broadcast_to(common, (16, 128))
        for c in xloads:
            c.wait()
    else:
        for c in xloads:
            c.start()
        out[...] = jnp.zeros_like(out)
        qload.wait()
        for c in xloads:
            c.wait()
        start_tiles()

    def input_gram(at):
        gram[at, :] = lax.dot_general(xs[at, :], qs[...], NT, preferred_element_type=F32)

    if not with_queries:
        @pl.loop(0, total // block)
        def _(b):
            input_gram(pl.ds(pl.multiple_of(b * block, block), block))

        wait_tiles()

    @pl.loop(0, total // block)
    def _(b):
        at = pl.ds(pl.multiple_of(b * block, block), block)
        if with_queries:
            input_gram(at)
        for j in range(TILES):
            cols = slice(256 * j, 256 * (j + 1))
            act, deriv = activations(jnp.dot(xs[at, :], ws[j], preferred_element_type=F32))
            part = fold(act * heads[:, cols])
            if j == 0:
                acc[at, :] = part
            else:
                acc[at, :] += part
            dv[:, cols] = deriv.astype(BF16)
        gram[at, :] = gram[at, :] * lax.dot_general(dv[...], qg[...], NT, preferred_element_type=F32)

    runs = []
    for i, (_, found) in enumerate(shapes):
        for row, count, side, relative, gx, gy, slot in found:
            place = lax.rem(x + gx + 4, 4) * 4 + lax.rem(y + gy + 4, 4) if relative else 4 * gx + gy
            runs.append((starts[i] + row, count, side, place, slot))
    for k, (row, count, side, place, slot) in enumerate(runs):
        length = info[8 + 2 * (place * 2 + 1 - core) + side]
        live = lax.broadcasted_iota(jnp.int32, (count, 1), 0) + slot < length
        live = jnp.where(live, 1.0 / jnp.maximum(length, 1).astype(F32), 0.0)
        sums_r[k:k + 1, :] = jnp.sum(acc[row:row + count, :] * live, axis=0, keepdims=True)
        sums_z[k:k + 1, :] = jnp.sum(gram[row:row + count, :] * live, axis=0, keepdims=True)
    reward = jnp.sum(sums_r[...], axis=1, keepdims=True)
    lanes = lax.broadcasted_iota(jnp.int32, (len(runs), 128), 1)
    tables = []
    for at in (0, SECOND):
        scores = jnp.dot(sums_z[...], pick(at), precision=HIGHEST, preferred_element_type=F32)
        tables.append(scores + jnp.where(lanes == at + REWARD, reward, 0.0))
    for k, (_, _, side, place, _) in enumerate(runs):
        at = pl.ds(place, 1)
        out[at, :] = out[at, :] + tables[side][k:k + 1, :]


ANY = pl.BlockSpec(memory_space=pl.ANY)
HBM = pl.BlockSpec(memory_space=pltpu.HBM)
VM = pl.BlockSpec(memory_space=pltpu.VMEM)
SM = pl.BlockSpec(memory_space=pltpu.SMEM)


def rows_call(rows, block, name, given, with_queries):
    xin = [r[0] for r in rows]
    shapes = tuple((v.shape, found) for v, found in rows)
    n = len(rows)
    total = sum(v.shape[0] for v in xin)
    runs = sum(len(found) for _, found in rows)
    out_shape = [jax.ShapeDtypeStruct((16, 128), F32)]
    if with_queries:
        out_shape += [jax.ShapeDtypeStruct((NQ, 2 * FD), BF16), jax.ShapeDtypeStruct((1, 2 * FD), F32)]
    return pl.pallas_call(
        functools.partial(rows_kernel, shapes, block, with_queries),
        out_shape=tuple(out_shape),
        in_specs=[HBM] * n + [SM] + [HBM] * 4 + [VM] * (3 if with_queries else 2),
        out_specs=(VM,) * len(out_shape),
        scratch_shapes=[
            pltpu.VMEM((total, D), BF16),
            pltpu.VMEM((NQ, D), BF16),
            pltpu.VMEM((TILES, D, 256), BF16),
            pltpu.VMEM((block, 2 * FD), BF16),
            pltpu.VMEM((total, 128), F32),
            pltpu.VMEM((total, 256), F32),
            pltpu.VMEM((runs, 128), F32),
            pltpu.VMEM((runs, 256), F32),
            pltpu.SemaphoreType.DMA((n,)),
            pltpu.SemaphoreType.DMA,
            pltpu.SemaphoreType.DMA((TILES, 2)),
        ],
        compiler_params=pltpu.CompilerParams(vmem_limit_bytes=56 * 2**20),
        cost_estimate=pl.CostEstimate(flops=1, bytes_accessed=1, transcendentals=0),
        name=name,
    )(*xin, *given)


def final_kernel(plane, got, out):
    rows = lax.broadcasted_iota(jnp.int32, (32, 128), 0)
    parts = []
    for zh in (0, 1):
        at = pl.ds(pl.multiple_of(64 * zh + 32 * (1 - plane[0]), 32), 32)
        v = got[at, :]
        for p in (0, 1):
            parts.append(jnp.sum(jnp.where((rows & 1) == p, v, 0.0), axis=0, keepdims=True))
    total = jnp.concatenate(parts, axis=0)
    lanes = lax.broadcasted_iota(jnp.int32, (4, 128), 1)
    at = lambda k: jnp.sum(jnp.where(lanes == k, total, 0.0), axis=1, keepdims=True)
    sigmoid = lambda v: 0.5 * jnp.tanh(0.5 * v) + 0.5
    factor = at(RATE) * (1.0 / 16.0) * sigmoid(at(SECOND + REWARD) - at(REWARD))
    for i in (0, 1):
        scores = [at(SECOND + 2 * i + k) - at(2 * i + k) for k in (0, 1)]
        value = factor * sigmoid(at(QUERY + 2 * i + 1) - at(QUERY + 2 * i)) * (scores[1] - scores[0])
        out[:, i:i + 1] = jnp.sum(value, axis=0, keepdims=True)


def final_call(plane, got):
    return pl.pallas_call(
        final_kernel,
        out_shape=jax.ShapeDtypeStruct((1, 2), F32),
        in_specs=[SM, VM],
        out_specs=VM,
        name="influence",
    )(plane, got)


def local(train_acts, train_len, query_acts, query_len, norm_gain, up_weight, readout, lr_weight):
    core, plane = lax.axis_index("c"), lax.axis_index("zl")
    x, y = lax.axis_index("x"), lax.axis_index("y")
    straight = core == plane
    turn = functools.partial(lax.ppermute, axis_name=("c", "zl"), perm=[(0, 2), (2, 3), (3, 1), (1, 0)])
    swap = functools.partial(lax.ppermute, axis_name="c", perm=[(0, 1), (1, 0)])
    low = lambda v, axis: lax.ppermute(v, axis, ring(1))
    high = lambda v, axis: lax.ppermute(v, axis, ring(-1))

    (query,) = norm_call(query_norm_kernel, (8,), query_acts[0], norm_gain)
    query_turned = turn(query)
    acts, _ = lax.optimization_barrier((train_acts[0], query))
    one, two, rest = norm_call(norm_kernel, (CP, CP, 2 * HEAD), acts, norm_gain)
    small = jnp.concatenate(
        [readout[0].astype(F32), jnp.zeros((RATE,), F32), lr_weight, jnp.zeros((127 - RATE,), F32)]
    ).reshape(1, FD + 128)
    query_turned, one = lax.optimization_barrier((query_turned, one))
    small_first, one, two, rest = turn(small), turn(one), turn(two), turn(rest)
    weight_own, small_first, one, two, rest = lax.optimization_barrier((up_weight[0], small_first, one, two, rest))
    weight_first = turn(weight_own)
    queries = lax.all_gather(query_turned, ("c", "x", "y"), axis=0, tiled=True)
    some = lax.all_gather(rest, ("x", "y"), axis=0, tiled=True)

    one_low, one_high = low(one, "x"), high(one, "x")
    two_low, two_high = low(two, "y"), high(two, "y")
    one_a, one_b = low(one_low[:32], "x"), high(one_high[32:], "x")
    two_a, two_b = low(two_low[:32], "y"), high(two_high[32:], "y")
    one_low, small_second = lax.optimization_barrier((one_low, swap(small_first)))
    moves = []
    for g in (0, 1):
        moves += [(5 * g, 0, 2 * g, 0, CP), (5 * g + 1, 0, 2 * g, CP, CP), (5 * g + 2, 0, 2 * g + 1, 0, CP),
                  (5 * g + 3, 0, 2 * g + 1, CP, 32), (5 * g + 4, 0, 2 * g + 1, CP + 32, 16)]
    a1, b1, a2, b2 = copy_call(
        (one, one_low, one_high, one_a, one_b, two, two_low, two_high, two_a, two_b), (2 * CP,) * 4, moves, "join_rows"
    )
    a1_low, b1_high = low(a1, "y"), high(b1, "y")
    a2_low, b2_high = low(a2, "x"), high(b2, "x")
    weight_first, a1_low, b1_high, a2_low, b2_high = lax.optimization_barrier(
        (weight_first, a1_low, b1_high, a2_low, b2_high)
    )
    weight_second = swap(weight_first)
    b1_low, a1_high = low(b1, "y"), high(a1, "y")
    b2_low, a2_high = low(b2, "x"), high(a2, "x")

    def group(*halves):
        found = []
        for side, g, ks in halves:
            for k in ks:
                gx, gy = (OFFS[k], OFFS[g]) if side == 0 else (OFFS[g], OFFS[k])
                found.append((CP * len(found), CP, side, True, gx, gy, HEAD))
        return tuple(found)

    gathered_runs = tuple(
        (HEAD * (2 * p + side), HEAD, side, False, p // 4, p % 4, 0) for p in range(16) for side in (0, 1)
    )
    near, far = (0, 1), (2, 3)
    info = jnp.concatenate([
        jnp.stack([straight.astype(jnp.int32), x, y, core]), query_len.reshape(-1), train_len.reshape(-1)
    ])
    given = (info, queries, weight_own, weight_first, weight_second)
    sums, *kept = rows_call(
        [(a1, group((0, 0, near))), (b1, group((0, 0, far))), (a2, group((1, 0, near))), (b2, group((1, 0, far))),
         (a1_low, group((0, 1, near))), (b1_high, group((0, 2, far))),
         (a2_low, group((1, 1, near))), (b2_high, group((1, 2, far)))],
        256, "first_rows", (*given, small, small_first, small_second), True,
    )
    sums, a1_on, b1_on, a2_on, b2_on = lax.optimization_barrier((sums, a1_low, b1_high, a2_low, b2_high))
    a1_far, b1_far = low(a1_on, "y"), high(b1_on, "y")
    a2_far, b2_far = low(a2_on, "x"), high(b2_on, "x")
    (more,) = rows_call(
        [(b1_low, group((0, 1, far))), (a1_high, group((0, 2, near))),
         (b2_low, group((1, 1, far))), (a2_high, group((1, 2, near))), (some, gathered_runs)],
        224, "next_rows", (*given, *kept), False,
    )
    (last,) = rows_call(
        [(a1_far, group((0, 3, near))), (b1_far, group((0, 3, far))),
         (a2_far, group((1, 3, near))), (b2_far, group((1, 3, far)))],
        192, "last_rows", (*given, *kept), False,
    )
    sums = sums + more + last
    message = jnp.broadcast_to(sums.reshape(1, 16, 1, 128), (4, 16, 2, 128)).reshape(128, 128)
    got = lax.all_to_all(message, ("zh", "c", "x", "y", "zl"), split_axis=0, concat_axis=0, tiled=True)
    return final_call(plane.reshape(1), got)


def solution(mesh):
    full = Mesh(mesh.devices.reshape(2, 2, 4, 4, 2), ("zh", "c", "x", "y", "zl"))
    ckpt, fsdp = ("zh", "c"), ("x", "y", "zl")
    return jax.shard_map(
        local,
        mesh=full,
        in_specs=(
            P(ckpt, fsdp, None),
            P(),
            P(ckpt, fsdp, None),
            P(),
            P(ckpt, None),
            P(ckpt, None, fsdp),
            P(ckpt, fsdp),
            P(ckpt),
        ),
        out_specs=P(fsdp, None),
        check_vma=False,
    )
```

```python
import functools

import jax
import jax.numpy as jnp
from jax import lax
from jax.experimental import pallas as pl
from jax.experimental.pallas import tpu as pltpu
from jax.sharding import Mesh
from jax.sharding import PartitionSpec as P

LEN = 64
D = 4096
FD = 640
TILES = 5
NQ = 256
OFFS = (0, -1, 1, 2)
F32 = jnp.float32
BF16 = jnp.bfloat16
NT = (((1,), (1,)), ((), ()))
HIGHEST = lax.Precision.HIGHEST
CP = 48
HEAD = LEN - CP
REWARD, SECOND, QUERY, RATE = 4, 8, 16, 20


def ring(step):
    return [(i, (i + step) % 4) for i in range(4)]


def activations(h):
    sig = 0.5 * jnp.tanh(0.5 * h) + 0.5
    act = h * sig
    return act, sig + act * (1.0 - sig)


def fold(v):
    return v[:, :128] + v[:, 128:]


def norm(v, gain):
    v = v.astype(F32)
    scale = lax.rsqrt(jnp.mean(v * v, axis=-1, keepdims=True) + 1e-05)
    return (v * scale * gain[...].astype(F32)).astype(BF16)


def query_norm_kernel(query, gain, out):
    out[...] = norm(query[...], gain)


def norm_kernel(acts, gain, both, rest):
    both[:CP, :] = norm(acts[HEAD:LEN, :], gain)
    both[CP:, :] = norm(acts[LEN + HEAD:, :], gain)
    rest[0:HEAD, :] = norm(acts[:HEAD, :], gain)
    rest[HEAD:, :] = norm(acts[LEN:LEN + HEAD, :], gain)


def norm_call(body, rows, acts, gain):
    return pl.pallas_call(
        body,
        out_shape=tuple(jax.ShapeDtypeStruct((n, D), BF16) for n in rows),
        in_specs=[VM] * 2,
        out_specs=(VM,) * len(rows),
        cost_estimate=pl.CostEstimate(flops=4 * sum(rows) * D, bytes_accessed=4 * sum(rows) * D, transcendentals=sum(rows)),
        name="norm_rows",
    )(acts, gain)


def copy_kernel(moves, n, m, *refs):
    src, dst, sem = refs[:n], refs[n:n + m], refs[n + m]
    copies = [
        pltpu.make_async_copy(src[i].at[pl.ds(s, k)], dst[o].at[pl.ds(d, k)], sem.at[c])
        for c, (i, s, o, d, k) in enumerate(moves)
    ]
    for c in copies:
        c.start()
    for c in copies:
        c.wait()


def copy_call(parts, rows, moves, name):
    return pl.pallas_call(
        functools.partial(copy_kernel, moves, len(parts), len(rows)),
        out_shape=tuple(jax.ShapeDtypeStruct((n, D), BF16) for n in rows),
        in_specs=[ANY] * len(parts),
        out_specs=(VM,) * len(rows),
        scratch_shapes=[pltpu.SemaphoreType.DMA((len(moves),))],
        cost_estimate=pl.CostEstimate(flops=0, bytes_accessed=sum(rows) * D * 4, transcendentals=0),
        name=name,
    )(*parts)


def rows_kernel(shapes, block, with_queries, *refs):
    n = len(shapes)
    xin = refs[:n]
    info, queries, own, first, second = refs[n:n + 5]
    if with_queries:
        small, small_first, small_second, out, qg, heads = refs[n + 5:n + 11]
    else:
        qg, heads, out = refs[n + 5:n + 8]
    xs, qs, ws, dv, acc, gram, sums_r, sums_z, xsem, qsem, wsem = refs[-11:]
    straight = info[0] == 1
    x, y, core = info[1], info[2], info[3]

    starts, xloads, at = [], [], 0
    for i, (shape, _) in enumerate(shapes):
        starts.append(at)
        xloads.append(pltpu.make_async_copy(xin[i], xs.at[pl.ds(at, shape[0])], xsem.at[i]))
        at += shape[0]
    total = at

    u = lax.broadcasted_iota(jnp.int32, (NQ, 128), 0)
    lane = lax.broadcasted_iota(jnp.int32, (NQ, 128), 1)
    qx, qy = (u >> 5) & 3, (u >> 3) & 3
    position = 8 * (2 * qy + jnp.where(u < 128, 1, 0)) + (u & 7)
    length = jnp.zeros((NQ, 128), jnp.int32)
    for k in range(4):
        length = jnp.where(qx == k, info[4 + k], length)
    weight = jnp.where(position < length, 1.0 / jnp.maximum(length, 1).astype(F32), 0.0)

    def pick(at):
        return jnp.where(qx == lane - at, weight, 0.0)

    qloads = [
        pltpu.make_async_copy(queries.at[pl.ds(64 * i, 64)], qs.at[pl.ds(64 * i, 64)], qsem.at[i]) for i in range(4)
    ]

    def tiles(a, b):
        moves = []
        for j in range(TILES):
            cols = pl.ds(128 * j, 128)
            for h, side in enumerate((a, b)):
                dst = ws.at[j, :, pl.ds(128 * h, 128)]
                moves.append(pltpu.make_async_copy(side.at[:, cols], dst, wsem.at[j, h]))
        return moves

    def start_tiles():
        @pl.when(straight)
        def _():
            for c in tiles(own, first):
                c.start()

        @pl.when(jnp.logical_not(straight))
        def _():
            for c in tiles(first, second):
                c.start()

    def wait_tiles():
        for c in tiles(first, second):
            c.wait()

    for c in qloads:
        c.start()
    if with_queries:
        start_tiles()
        for j in range(TILES):
            cols = slice(128 * j, 128 * (j + 1))
            heads[:, 256 * j:256 * j + 128] = jnp.where(straight, small[:, cols], small_first[:, cols])
            heads[:, 256 * j + 128:256 * j + 256] = jnp.where(straight, small_first[:, cols], small_second[:, cols])
        for c in qloads:
            c.wait()
        wait_tiles()
        for c in xloads:
            c.start()
        query_total = None
        for j in range(TILES):
            row = heads[:, 256 * j:256 * (j + 1)]
            act, deriv = activations(jnp.dot(qs[...], ws[j], preferred_element_type=F32))
            part = fold(act * row)
            query_total = part if j == 0 else query_total + part
            qg[:, 256 * j:256 * (j + 1)] = (row * row * deriv).astype(BF16)
        common = jnp.sum(jnp.sum(query_total, axis=1, keepdims=True) * pick(QUERY), axis=0, keepdims=True)
        common += jnp.where(straight, small[:, FD:], small_first[:, FD:])
        out[...] = jnp.broadcast_to(common, (16, 128))
        for c in xloads:
            c.wait()
    else:
        for c in xloads:
            c.start()
        out[...] = jnp.zeros_like(out)
        for c in qloads + xloads:
            c.wait()
        start_tiles()

    def input_gram(at):
        gram[at, :] = lax.dot_general(xs[at, :], qs[...], NT, preferred_element_type=F32)

    if not with_queries:
        @pl.loop(0, total // block)
        def _(b):
            input_gram(pl.ds(pl.multiple_of(b * block, block), block))

        wait_tiles()

    @pl.loop(0, total // block)
    def _(b):
        at = pl.ds(pl.multiple_of(b * block, block), block)
        if with_queries:
            input_gram(at)
        for j in range(TILES):
            cols = slice(256 * j, 256 * (j + 1))
            act, deriv = activations(jnp.dot(xs[at, :], ws[j], preferred_element_type=F32))
            part = fold(act * heads[:, cols])
            if j == 0:
                acc[at, :] = part
            else:
                acc[at, :] += part
            dv[:, cols] = deriv.astype(BF16)
        gram[at, :] = gram[at, :] * lax.dot_general(dv[...], qg[...], NT, preferred_element_type=F32)

    runs = []
    for i, (_, found) in enumerate(shapes):
        for row, count, side, relative, gx, gy, slot in found:
            place = lax.rem(x + gx + 4, 4) * 4 + lax.rem(y + gy + 4, 4) if relative else 4 * gx + gy
            runs.append((starts[i] + row, count, side, place, slot))
    for k, (row, count, side, place, slot) in enumerate(runs):
        length = info[8 + 2 * (place * 2 + 1 - core) + side]
        live = lax.broadcasted_iota(jnp.int32, (count, 1), 0) + slot < length
        live = jnp.where(live, 1.0 / jnp.maximum(length, 1).astype(F32), 0.0)
        sums_r[k:k + 1, :] = jnp.sum(acc[row:row + count, :] * live, axis=0, keepdims=True)
        sums_z[k:k + 1, :] = jnp.sum(gram[row:row + count, :] * live, axis=0, keepdims=True)
    reward = jnp.sum(sums_r[...], axis=1, keepdims=True)
    lanes = lax.broadcasted_iota(jnp.int32, (len(runs), 128), 1)
    tables = []
    for at in (0, SECOND):
        scores = jnp.dot(sums_z[...], pick(at), precision=HIGHEST, preferred_element_type=F32)
        tables.append(scores + jnp.where(lanes == at + REWARD, reward, 0.0))
    for k, (_, _, side, place, _) in enumerate(runs):
        at = pl.ds(place, 1)
        out[at, :] = out[at, :] + tables[side][k:k + 1, :]


ANY = pl.BlockSpec(memory_space=pl.ANY)
HBM = pl.BlockSpec(memory_space=pltpu.HBM)
VM = pl.BlockSpec(memory_space=pltpu.VMEM)
SM = pl.BlockSpec(memory_space=pltpu.SMEM)


def rows_call(rows, block, name, given, with_queries, space=HBM, limit=56):
    xin = [r[0] for r in rows]
    shapes = tuple((v.shape, found) for v, found in rows)
    n = len(rows)
    total = sum(v.shape[0] for v in xin)
    runs = sum(len(found) for _, found in rows)
    out_shape = [jax.ShapeDtypeStruct((16, 128), F32)]
    if with_queries:
        out_shape += [jax.ShapeDtypeStruct((NQ, 2 * FD), BF16), jax.ShapeDtypeStruct((1, 2 * FD), F32)]
    return pl.pallas_call(
        functools.partial(rows_kernel, shapes, block, with_queries),
        out_shape=tuple(out_shape),
        in_specs=[space] * n + [SM] + [HBM] * 4 + [VM] * (3 if with_queries else 2),
        out_specs=(VM,) * len(out_shape),
        scratch_shapes=[
            pltpu.VMEM((total, D), BF16),
            pltpu.VMEM((NQ, D), BF16),
            pltpu.VMEM((TILES, D, 256), BF16),
            pltpu.VMEM((block, 2 * FD), BF16),
            pltpu.VMEM((total, 128), F32),
            pltpu.VMEM((total, 256), F32),
            pltpu.VMEM((runs, 128), F32),
            pltpu.VMEM((runs, 256), F32),
            pltpu.SemaphoreType.DMA((n,)),
            pltpu.SemaphoreType.DMA((4,)),
            pltpu.SemaphoreType.DMA((TILES, 2)),
        ],
        compiler_params=pltpu.CompilerParams(vmem_limit_bytes=limit * 2**20),
        cost_estimate=pl.CostEstimate(flops=1, bytes_accessed=1, transcendentals=0),
        name=name,
    )(*xin, *given)


def final_kernel(plane, got, out):
    rows = lax.broadcasted_iota(jnp.int32, (32, 128), 0)
    parts = []
    for zh in (0, 1):
        at = pl.ds(pl.multiple_of(64 * zh + 32 * (1 - plane[0]), 32), 32)
        v = got[at, :]
        for p in (0, 1):
            parts.append(jnp.sum(jnp.where((rows & 1) == p, v, 0.0), axis=0, keepdims=True))
    total = jnp.concatenate(parts, axis=0)
    lanes = lax.broadcasted_iota(jnp.int32, (4, 128), 1)
    at = lambda k: jnp.sum(jnp.where(lanes == k, total, 0.0), axis=1, keepdims=True)
    sigmoid = lambda v: 0.5 * jnp.tanh(0.5 * v) + 0.5
    factor = at(RATE) * (1.0 / 16.0) * sigmoid(at(SECOND + REWARD) - at(REWARD))
    for i in (0, 1):
        scores = [at(SECOND + 2 * i + k) - at(2 * i + k) for k in (0, 1)]
        value = factor * sigmoid(at(QUERY + 2 * i + 1) - at(QUERY + 2 * i)) * (scores[1] - scores[0])
        out[:, i:i + 1] = jnp.sum(value, axis=0, keepdims=True)


def final_call(plane, got):
    return pl.pallas_call(
        final_kernel,
        out_shape=jax.ShapeDtypeStruct((1, 2), F32),
        in_specs=[SM, VM],
        out_specs=VM,
        name="influence",
    )(plane, got)


def local(train_acts, train_len, query_acts, query_len, norm_gain, up_weight, readout, lr_weight):
    core, plane = lax.axis_index("c"), lax.axis_index("zl")
    x, y = lax.axis_index("x"), lax.axis_index("y")
    straight = core == plane
    turn = functools.partial(lax.ppermute, axis_name=("c", "zl"), perm=[(0, 2), (2, 3), (3, 1), (1, 0)])
    swap = functools.partial(lax.ppermute, axis_name="c", perm=[(0, 1), (1, 0)])
    low = lambda v, axis: lax.ppermute(v, axis, ring(1))
    high = lambda v, axis: lax.ppermute(v, axis, ring(-1))

    (query,) = norm_call(query_norm_kernel, (8,), query_acts[0], norm_gain)
    query_turned = turn(query)
    acts, _ = lax.optimization_barrier((train_acts[0], query))
    both, rest = norm_call(norm_kernel, (2 * CP, 2 * HEAD), acts, norm_gain)
    small = jnp.concatenate(
        [readout[0].astype(F32), jnp.zeros((RATE,), F32), lr_weight, jnp.zeros((127 - RATE,), F32)]
    ).reshape(1, FD + 128)
    query_turned, both = lax.optimization_barrier((query_turned, both))
    both, rest, small_first = turn(both), turn(rest), turn(small)
    weight_own, small_first, both, rest = lax.optimization_barrier((up_weight[0], small_first, both, rest))
    one, two = both[:CP], both[CP:]
    weight_first = turn(weight_own)
    queries = lax.all_gather(query_turned, ("c", "x", "y"), axis=0, tiled=True)
    some = lax.all_gather(rest, ("x", "y"), axis=0, tiled=True)

    one_low, one_high = low(one, "x"), high(one, "x")
    two_low, two_high = low(two, "y"), high(two, "y")
    one_a, one_b = low(one_low[:32], "x"), high(one_high[32:], "x")
    two_a, two_b = low(two_low[:32], "y"), high(two_high[32:], "y")
    one_low, small_second = lax.optimization_barrier((one_low, swap(small_first)))
    moves = []
    for g in (0, 1):
        moves += [(4 * 2, CP * g, 2 * g, 0, CP), (4 * g, 0, 2 * g, CP, CP), (4 * g + 1, 0, 2 * g + 1, 0, CP),
                  (4 * g + 2, 0, 2 * g + 1, CP, 32), (4 * g + 3, 0, 2 * g + 1, CP + 32, 16)]
    a1, b1, a2, b2 = copy_call(
        (one_low, one_high, one_a, one_b, two_low, two_high, two_a, two_b, both), (2 * CP,) * 4, moves, "join_rows"
    )
    a1_low, b1_high = low(a1, "y"), high(b1, "y")
    a2_low, b2_high = low(a2, "x"), high(b2, "x")
    weight_first, a1_low, b1_high, a2_low, b2_high = lax.optimization_barrier(
        (weight_first, a1_low, b1_high, a2_low, b2_high)
    )
    weight_second = swap(weight_first)
    b1_low, a1_high = low(b1, "y"), high(a1, "y")
    b2_low, a2_high = low(b2, "x"), high(a2, "x")

    def group(*halves):
        found = []
        for side, g, ks in halves:
            for k in ks:
                gx, gy = (OFFS[k], OFFS[g]) if side == 0 else (OFFS[g], OFFS[k])
                found.append((CP * len(found), CP, side, True, gx, gy, HEAD))
        return tuple(found)

    gathered_runs = tuple(
        (HEAD * (2 * p + side), HEAD, side, False, p // 4, p % 4, 0) for p in range(16) for side in (0, 1)
    )
    near, far = (0, 1), (2, 3)
    info = jnp.concatenate([
        jnp.stack([straight.astype(jnp.int32), x, y, core]), query_len.reshape(-1), train_len.reshape(-1)
    ])
    given = (info, queries, weight_own, weight_first, weight_second)
    sums, *kept = rows_call(
        [(a1, group((0, 0, near))), (b1, group((0, 0, far))), (a2, group((1, 0, near))), (b2, group((1, 0, far))),
         (a1_low, group((0, 1, near))), (b1_high, group((0, 2, far))),
         (a2_low, group((1, 1, near))), (b2_high, group((1, 2, far)))],
        256, "first_rows", (*given, small, small_first, small_second), True,
    )
    sums, a1_on, b1_on, a2_on, b2_on = lax.optimization_barrier((sums, a1_low, b1_high, a2_low, b2_high))
    a1_far, b1_far = low(a1_on, "y"), high(b1_on, "y")
    a2_far, b2_far = low(a2_on, "x"), high(b2_on, "x")
    (more,) = rows_call(
        [(b1_low, group((0, 1, far))), (a1_high, group((0, 2, near))),
         (b2_low, group((1, 1, far))), (a2_high, group((1, 2, near))), (some, gathered_runs)],
        224, "next_rows", (*given, *kept), False,
    )
    (last,) = rows_call(
        [(a1_far, group((0, 3, near))), (b1_far, group((0, 3, far))),
         (a2_far, group((1, 3, near))), (b2_far, group((1, 3, far)))],
        192, "last_rows", (*given, *kept), False, ANY, 30,
    )
    sums = sums + more + last
    message = jnp.broadcast_to(sums.reshape(1, 16, 1, 128), (4, 16, 2, 128)).reshape(128, 128)
    got = lax.all_to_all(message, ("zh", "c", "x", "y", "zl"), split_axis=0, concat_axis=0, tiled=True)
    return final_call(plane.reshape(1), got)


def solution(mesh):
    full = Mesh(mesh.devices.reshape(2, 2, 4, 4, 2), ("zh", "c", "x", "y", "zl"))
    ckpt, fsdp = ("zh", "c"), ("x", "y", "zl")
    return jax.shard_map(
        local,
        mesh=full,
        in_specs=(
            P(ckpt, fsdp, None),
            P(),
            P(ckpt, fsdp, None),
            P(),
            P(ckpt, None),
            P(ckpt, None, fsdp),
            P(ckpt, fsdp),
            P(ckpt),
        ),
        out_specs=P(fsdp, None),
        check_vma=False,
    )
```

```python
import functools

import jax
import jax.numpy as jnp
from jax import lax
from jax.experimental import pallas as pl
from jax.experimental.pallas import tpu as pltpu
from jax.sharding import Mesh
from jax.sharding import PartitionSpec as P

LEN = 64
D = 4096
FD = 640
TILES = 5
NQ = 256
OFFS = (0, -1, 1, 2)
F32 = jnp.float32
BF16 = jnp.bfloat16
NT = (((1,), (1,)), ((), ()))
HIGHEST = lax.Precision.HIGHEST
CP = 48
HEAD = LEN - CP
REWARD, SECOND, QUERY, RATE = 4, 8, 16, 20


def ring(step):
    return [(i, (i + step) % 4) for i in range(4)]


def activations(h):
    sig = 0.5 * jnp.tanh(0.5 * h) + 0.5
    act = h * sig
    return act, sig + act * (1.0 - sig)


def fold(v):
    return v[:, :128] + v[:, 128:]


def norm(v, gain):
    v = v.astype(F32)
    scale = lax.rsqrt(jnp.mean(v * v, axis=-1, keepdims=True) + 1e-05)
    return (v * scale * gain[...].astype(F32)).astype(BF16)


def query_norm_kernel(query, gain, out):
    out[...] = norm(query[...], gain)


def norm_kernel(acts, gain, both, rest):
    both[:CP, :] = norm(acts[HEAD:LEN, :], gain)
    both[CP:, :] = norm(acts[LEN + HEAD:, :], gain)
    rest[0:HEAD, :] = norm(acts[:HEAD, :], gain)
    rest[HEAD:, :] = norm(acts[LEN:LEN + HEAD, :], gain)


def norm_call(body, rows, acts, gain):
    return pl.pallas_call(
        body,
        out_shape=tuple(jax.ShapeDtypeStruct((n, D), BF16) for n in rows),
        in_specs=[VM] * 2,
        out_specs=(VM,) * len(rows),
        cost_estimate=pl.CostEstimate(flops=4 * sum(rows) * D, bytes_accessed=4 * sum(rows) * D, transcendentals=sum(rows)),
        name="norm_rows",
    )(acts, gain)


def copy_kernel(moves, n, m, *refs):
    src, dst, sem = refs[:n], refs[n:n + m], refs[n + m]
    copies = [
        pltpu.make_async_copy(src[i].at[pl.ds(s, k)], dst[o].at[pl.ds(d, k)], sem.at[c])
        for c, (i, s, o, d, k) in enumerate(moves)
    ]
    for c in copies:
        c.start()
    for c in copies:
        c.wait()


def copy_call(parts, rows, moves, name):
    return pl.pallas_call(
        functools.partial(copy_kernel, moves, len(parts), len(rows)),
        out_shape=tuple(jax.ShapeDtypeStruct((n, D), BF16) for n in rows),
        in_specs=[ANY] * len(parts),
        out_specs=(VM,) * len(rows),
        scratch_shapes=[pltpu.SemaphoreType.DMA((len(moves),))],
        cost_estimate=pl.CostEstimate(flops=0, bytes_accessed=sum(rows) * D * 4, transcendentals=0),
        name=name,
    )(*parts)


def rows_kernel(shapes, block, with_queries, *refs):
    n = len(shapes)
    xin = refs[:n]
    info, queries, own, first, second = refs[n:n + 5]
    if with_queries:
        small, small_first, small_second, out, qg, heads = refs[n + 5:n + 11]
    else:
        qg, heads, out = refs[n + 5:n + 8]
    xs, qs, ws, dv, acc, gram, sums_r, sums_z, xsem, qsem, wsem = refs[-11:]
    straight = info[0] == 1
    x, y, core = info[1], info[2], info[3]

    starts, xloads, at = [], [], 0
    for i, (shape, _) in enumerate(shapes):
        starts.append(at)
        xloads.append(pltpu.make_async_copy(xin[i], xs.at[pl.ds(at, shape[0])], xsem.at[i]))
        at += shape[0]
    total = at

    u = lax.broadcasted_iota(jnp.int32, (NQ, 128), 0)
    lane = lax.broadcasted_iota(jnp.int32, (NQ, 128), 1)
    qx, qy = (u >> 5) & 3, (u >> 3) & 3
    position = 8 * (2 * qy + jnp.where(u < 128, 1, 0)) + (u & 7)
    length = jnp.zeros((NQ, 128), jnp.int32)
    for k in range(4):
        length = jnp.where(qx == k, info[4 + k], length)
    weight = jnp.where(position < length, 1.0 / jnp.maximum(length, 1).astype(F32), 0.0)

    def pick(at):
        return jnp.where(qx == lane - at, weight, 0.0)

    qloads = [
        pltpu.make_async_copy(queries.at[pl.ds(64 * i, 64)], qs.at[pl.ds(64 * i, 64)], qsem.at[i]) for i in range(4)
    ]

    def tiles(a, b):
        moves = []
        for j in range(TILES):
            cols = pl.ds(128 * j, 128)
            for h, side in enumerate((a, b)):
                dst = ws.at[j, :, pl.ds(128 * h, 128)]
                moves.append(pltpu.make_async_copy(side.at[:, cols], dst, wsem.at[j, h]))
        return moves

    def start_tiles():
        @pl.when(straight)
        def _():
            for c in tiles(own, first):
                c.start()

        @pl.when(jnp.logical_not(straight))
        def _():
            for c in tiles(first, second):
                c.start()

    def wait_tiles():
        for c in tiles(first, second):
            c.wait()

    for c in qloads:
        c.start()
    if with_queries:
        start_tiles()
        for j in range(TILES):
            cols = slice(128 * j, 128 * (j + 1))
            heads[:, 256 * j:256 * j + 128] = jnp.where(straight, small[:, cols], small_first[:, cols])
            heads[:, 256 * j + 128:256 * j + 256] = jnp.where(straight, small_first[:, cols], small_second[:, cols])
        for c in qloads:
            c.wait()
        wait_tiles()
        for c in xloads:
            c.start()
        query_total = None
        for j in range(TILES):
            row = heads[:, 256 * j:256 * (j + 1)]
            act, deriv = activations(jnp.dot(qs[...], ws[j], preferred_element_type=F32))
            part = fold(act * row)
            query_total = part if j == 0 else query_total + part
            qg[:, 256 * j:256 * (j + 1)] = (row * row * deriv).astype(BF16)
        common = jnp.sum(jnp.sum(query_total, axis=1, keepdims=True) * pick(QUERY), axis=0, keepdims=True)
        common += jnp.where(straight, small[:, FD:], small_first[:, FD:])
        out[...] = jnp.broadcast_to(common, (16, 128))
        for c in xloads:
            c.wait()
    else:
        for c in xloads:
            c.start()
        out[...] = jnp.zeros_like(out)
        for c in qloads + xloads:
            c.wait()
        start_tiles()

    def input_gram(at):
        gram[at, :] = lax.dot_general(xs[at, :], qs[...], NT, preferred_element_type=F32)

    if not with_queries:
        @pl.loop(0, total // block)
        def _(b):
            input_gram(pl.ds(pl.multiple_of(b * block, block), block))

        wait_tiles()

    @pl.loop(0, total // block)
    def _(b):
        at = pl.ds(pl.multiple_of(b * block, block), block)
        if with_queries:
            input_gram(at)
        for j in range(TILES):
            cols = slice(256 * j, 256 * (j + 1))
            act, deriv = activations(jnp.dot(xs[at, :], ws[j], preferred_element_type=F32))
            part = fold(act * heads[:, cols])
            if j == 0:
                acc[at, :] = part
            else:
                acc[at, :] += part
            dv[:, cols] = deriv.astype(BF16)
        gram[at, :] = gram[at, :] * lax.dot_general(dv[...], qg[...], NT, preferred_element_type=F32)

    runs = []
    for i, (_, found) in enumerate(shapes):
        for row, count, side, relative, gx, gy, slot in found:
            place = lax.rem(x + gx + 4, 4) * 4 + lax.rem(y + gy + 4, 4) if relative else 4 * gx + gy
            runs.append((starts[i] + row, count, side, place, slot))
    for k, (row, count, side, place, slot) in enumerate(runs):
        length = info[8 + 2 * (place * 2 + 1 - core) + side]
        live = lax.broadcasted_iota(jnp.int32, (count, 1), 0) + slot < length
        live = jnp.where(live, 1.0 / jnp.maximum(length, 1).astype(F32), 0.0)
        sums_r[k:k + 1, :] = jnp.sum(acc[row:row + count, :] * live, axis=0, keepdims=True)
        sums_z[k:k + 1, :] = jnp.sum(gram[row:row + count, :] * live, axis=0, keepdims=True)
    reward = jnp.sum(sums_r[...], axis=1, keepdims=True)
    lanes = lax.broadcasted_iota(jnp.int32, (len(runs), 128), 1)
    tables = []
    for at in (0, SECOND):
        scores = jnp.dot(sums_z[...], pick(at), precision=HIGHEST, preferred_element_type=F32)
        tables.append(scores + jnp.where(lanes == at + REWARD, reward, 0.0))
    for k, (_, _, side, place, _) in enumerate(runs):
        at = pl.ds(place, 1)
        out[at, :] = out[at, :] + tables[side][k:k + 1, :]


ANY = pl.BlockSpec(memory_space=pl.ANY)
HBM = pl.BlockSpec(memory_space=pltpu.HBM)
VM = pl.BlockSpec(memory_space=pltpu.VMEM)
SM = pl.BlockSpec(memory_space=pltpu.SMEM)


def rows_call(rows, block, name, given, with_queries, space=HBM, limit=56):
    xin = [r[0] for r in rows]
    shapes = tuple((v.shape, found) for v, found in rows)
    n = len(rows)
    total = sum(v.shape[0] for v in xin)
    runs = sum(len(found) for _, found in rows)
    out_shape = [jax.ShapeDtypeStruct((16, 128), F32)]
    if with_queries:
        out_shape += [jax.ShapeDtypeStruct((NQ, 2 * FD), BF16), jax.ShapeDtypeStruct((1, 2 * FD), F32)]
    return pl.pallas_call(
        functools.partial(rows_kernel, shapes, block, with_queries),
        out_shape=tuple(out_shape),
        in_specs=[space] * n + [SM] + [HBM] * 4 + [VM] * (3 if with_queries else 2),
        out_specs=(VM,) * len(out_shape),
        scratch_shapes=[
            pltpu.VMEM((total, D), BF16),
            pltpu.VMEM((NQ, D), BF16),
            pltpu.VMEM((TILES, D, 256), BF16),
            pltpu.VMEM((block, 2 * FD), BF16),
            pltpu.VMEM((total, 128), F32),
            pltpu.VMEM((total, 256), F32),
            pltpu.VMEM((runs, 128), F32),
            pltpu.VMEM((runs, 256), F32),
            pltpu.SemaphoreType.DMA((n,)),
            pltpu.SemaphoreType.DMA((4,)),
            pltpu.SemaphoreType.DMA((TILES, 2)),
        ],
        compiler_params=pltpu.CompilerParams(vmem_limit_bytes=limit * 2**20),
        cost_estimate=pl.CostEstimate(flops=1, bytes_accessed=1, transcendentals=0),
        name=name,
    )(*xin, *given)


def final_kernel(plane, got, out):
    rows = lax.broadcasted_iota(jnp.int32, (32, 128), 0)
    parts = []
    for zh in (0, 1):
        at = pl.ds(pl.multiple_of(64 * zh + 32 * (1 - plane[0]), 32), 32)
        v = got[at, :]
        for p in (0, 1):
            parts.append(jnp.sum(jnp.where((rows & 1) == p, v, 0.0), axis=0, keepdims=True))
    total = jnp.concatenate(parts, axis=0)
    lanes = lax.broadcasted_iota(jnp.int32, (4, 128), 1)
    at = lambda k: jnp.sum(jnp.where(lanes == k, total, 0.0), axis=1, keepdims=True)
    sigmoid = lambda v: 0.5 * jnp.tanh(0.5 * v) + 0.5
    factor = at(RATE) * (1.0 / 16.0) * sigmoid(at(SECOND + REWARD) - at(REWARD))
    for i in (0, 1):
        scores = [at(SECOND + 2 * i + k) - at(2 * i + k) for k in (0, 1)]
        value = factor * sigmoid(at(QUERY + 2 * i + 1) - at(QUERY + 2 * i)) * (scores[1] - scores[0])
        out[:, i:i + 1] = jnp.sum(value, axis=0, keepdims=True)


def final_call(plane, got):
    return pl.pallas_call(
        final_kernel,
        out_shape=jax.ShapeDtypeStruct((1, 2), F32),
        in_specs=[SM, VM],
        out_specs=VM,
        name="influence",
    )(plane, got)


def local(train_acts, train_len, query_acts, query_len, norm_gain, up_weight, readout, lr_weight):
    core, plane = lax.axis_index("c"), lax.axis_index("zl")
    x, y = lax.axis_index("x"), lax.axis_index("y")
    straight = core == plane
    turn = functools.partial(lax.ppermute, axis_name=("c", "zl"), perm=[(0, 2), (2, 3), (3, 1), (1, 0)])
    swap = functools.partial(lax.ppermute, axis_name="c", perm=[(0, 1), (1, 0)])
    low = lambda v, axis: lax.ppermute(v, axis, ring(1))
    high = lambda v, axis: lax.ppermute(v, axis, ring(-1))

    (query,) = norm_call(query_norm_kernel, (8,), query_acts[0], norm_gain)
    query_turned = turn(query)
    acts, _ = lax.optimization_barrier((train_acts[0], query))
    both, rest = norm_call(norm_kernel, (2 * CP, 2 * HEAD), acts, norm_gain)
    small = jnp.concatenate(
        [readout[0].astype(F32), jnp.zeros((RATE,), F32), lr_weight, jnp.zeros((127 - RATE,), F32)]
    ).reshape(1, FD + 128)
    query_turned, both = lax.optimization_barrier((query_turned, both))
    both, rest, small_first = turn(both), turn(rest), turn(small)
    weight_own, small_first, both, rest = lax.optimization_barrier((up_weight[0], small_first, both, rest))
    one, two = both[:CP], both[CP:]
    weight_first = turn(weight_own)
    queries = lax.all_gather(query_turned, ("c", "x", "y"), axis=0, tiled=True)
    some = lax.all_gather(rest, ("x", "y"), axis=0, tiled=True)

    one_low, one_high = low(one, "x"), high(one, "x")
    two_low, two_high = low(two, "y"), high(two, "y")
    one_a, one_b = low(one_low[:32], "x"), high(one_high[32:], "x")
    two_a, two_b = low(two_low[:32], "y"), high(two_high[32:], "y")
    one_low, small_second = lax.optimization_barrier((one_low, swap(small_first)))
    moves = []
    for g in (0, 1):
        moves += [(4 * 2, CP * g, 2 * g, 0, CP), (4 * g, 0, 2 * g, CP, CP), (4 * g + 1, 0, 2 * g + 1, 0, CP),
                  (4 * g + 2, 0, 2 * g + 1, CP, 32), (4 * g + 3, 0, 2 * g + 1, CP + 32, 16)]
    a1, b1, a2, b2 = copy_call(
        (one_low, one_high, one_a, one_b, two_low, two_high, two_a, two_b, both), (2 * CP,) * 4, moves, "join_rows"
    )
    a1_low, b1_high = low(a1, "y"), high(b1, "y")
    a2_low, b2_high = low(a2, "x"), high(b2, "x")
    weight_first, a1_low, b1_high, a2_low, b2_high = lax.optimization_barrier(
        (weight_first, a1_low, b1_high, a2_low, b2_high)
    )
    weight_second = swap(weight_first)
    b1_low, a1_high = low(b1, "y"), high(a1, "y")
    b2_low, a2_high = low(b2, "x"), high(a2, "x")

    def group(*halves):
        found = []
        for side, g, ks in halves:
            for k in ks:
                gx, gy = (OFFS[k], OFFS[g]) if side == 0 else (OFFS[g], OFFS[k])
                found.append((CP * len(found), CP, side, True, gx, gy, HEAD))
        return tuple(found)

    gathered_runs = tuple(
        (HEAD * (2 * p + side), HEAD, side, False, p // 4, p % 4, 0) for p in range(16) for side in (0, 1)
    )
    near, far = (0, 1), (2, 3)
    info = jnp.concatenate([
        jnp.stack([straight.astype(jnp.int32), x, y, core]), query_len.reshape(-1), train_len.reshape(-1)
    ])
    given = (info, queries, weight_own, weight_first, weight_second)
    sums, *kept = rows_call(
        [(a1, group((0, 0, near))), (b1, group((0, 0, far))), (a2, group((1, 0, near))), (b2, group((1, 0, far))),
         (a1_low, group((0, 1, near))), (b1_high, group((0, 2, far))),
         (a2_low, group((1, 1, near))), (b2_high, group((1, 2, far)))],
        256, "first_rows", (*given, small, small_first, small_second), True,
    )
    sums, a1_on, b1_on, a2_on, b2_on = lax.optimization_barrier((sums, a1_low, b1_high, a2_low, b2_high))
    a1_far, b1_far = low(a1_on, "y"), high(b1_on, "y")
    a2_far, b2_far = low(a2_on, "x"), high(b2_on, "x")
    (more,) = rows_call(
        [(b1_low, group((0, 1, far))), (a1_high, group((0, 2, near))),
         (b2_low, group((1, 1, far))), (a2_high, group((1, 2, near))), (some, gathered_runs)],
        224, "next_rows", (*given, *kept), False, HBM, 48,
    )
    (last,) = rows_call(
        [(a1_far, group((0, 3, near))), (b1_far, group((0, 3, far))),
         (a2_far, group((1, 3, near))), (b2_far, group((1, 3, far)))],
        192, "last_rows", (*given, *kept), False, ANY, 30,
    )
    sums = sums + more + last
    message = jnp.broadcast_to(sums.reshape(1, 16, 1, 128), (4, 16, 2, 128)).reshape(128, 128)
    got = lax.all_to_all(message, ("zh", "c", "x", "y", "zl"), split_axis=0, concat_axis=0, tiled=True)
    return final_call(plane.reshape(1), got)


def solution(mesh):
    full = Mesh(mesh.devices.reshape(2, 2, 4, 4, 2), ("zh", "c", "x", "y", "zl"))
    ckpt, fsdp = ("zh", "c"), ("x", "y", "zl")
    return jax.shard_map(
        local,
        mesh=full,
        in_specs=(
            P(ckpt, fsdp, None),
            P(),
            P(ckpt, fsdp, None),
            P(),
            P(ckpt, None),
            P(ckpt, None, fsdp),
            P(ckpt, fsdp),
            P(ckpt),
        ),
        out_specs=P(fsdp, None),
        check_vma=False,
    )
```
